32 devices in a mesh: row: 16 (over z, x, core), col: 2 (over y).
Axes of the slice: x: 2, y: 2, z: 4, core: 2. Of those that a mesh axis runs over, the one named last changes fastest.
Arguments:
- eigvecs: float32 [4096, 2048], P('row', 'col'), may hold values from -6 to 6
- panels: float32 [5, 16, 256, 128], P(None, 'row', 'col'), may hold values from -6 to 6
- sweep_shift: int32 [5], replicated, may hold values from 0 to 15
- slot_group: int32 [5, 16], replicated, may hold values from 0 to 15, each once within a row
Outputs:
- full_vectors: float32 [4096, 2048], P('row', 'col')
The draws below stay inside these ranges and needn't reach their ends.
Inputs may be any that keep to these rules, and one draw needn't show every extreme that they name: Each row of slot_group names each of the 16 groups once.
All inputs are finite; a program needn't handle non-finite values.
Results may differ from the reference program's by a relative error of at most 0.00029.
Values sent between devices are 32-bit elements; how exact they have to be, the bound alone decides.
No kernel may reach another device: no remote copies, remote signals or barrier semaphores. Data moves between devices by JAX's collectives and lax.ppermute only.
A program may use at most 128 MiB of HBM per device.

```python
import jax
import jax.numpy as jnp
from jax import lax

B = 128
SWEEPS = 5
W = 256
NROWS = 4096
NCOLS = 2048
NG = 16


def set_ends(drawn, own_key, least, top_value):
    dims = drawn.shape
    index_at = [jax.random.randint(jax.random.fold_in(own_key, axis), (), 0, dims[axis]) for axis in range(len(dims))]
    drawn = drawn.at[tuple(index_at)].set(least)
    longest = dims.index(max(dims))
    index_at[longest] = (index_at[longest] + 1) % dims[longest]
    return drawn.at[tuple(index_at)].set(top_value)


def block_levels(key, shape, pieces, smallest, largest):
    gain, own = 1.0, jax.random.fold_in(key, 6)
    for position, shards_of in pieces:
        draws = jnp.exp(jax.random.uniform(jax.random.fold_in(own, position), (shards_of,), jnp.float32, smallest / len(pieces), largest / len(pieces)))
        gain = gain * jnp.repeat(draws, shape[position] // shards_of).reshape([-1 if axis == position else 1 for axis in range(len(shape))])
    return gain


def noise(key, shape, width, most, shards=(), held_as=jnp.bfloat16):
    drawn = width * jax.random.normal(key, shape, jnp.float32)
    if shards:
        drawn = drawn * block_levels(key, shape, shards, -0.22, 0.18)
    return jnp.clip(drawn, -most, most).astype(held_as)


def setup_inputs(seed: int = 0) -> dict:
    splits = jax.random.split(jax.random.key(seed), 5)
    return {
        "eigvecs": noise(splits[0], (NROWS, NCOLS), 1.0, 6.0, ((0, 16), (1, 2)), jnp.float32),
        "panels": noise(splits[1], (SWEEPS, NG, W, B), 1.0, 6.0, ((1, 16), (2, 2)), jnp.float32),
        "sweep_shift": set_ends(jax.random.randint(splits[2], (SWEEPS,), 0, NG), jax.random.fold_in(splits[2], 1), 0, NG - 1).astype(jnp.int32),
        "slot_group": jax.vmap(lambda own: jax.random.permutation(own, NG))(jax.random.split(splits[3], SWEEPS)).reshape((SWEEPS, NG)).astype(jnp.int32),
    }


PRECISE = lax.Precision.HIGHEST

def apply_groups(vectors, windows):
    products = jnp.einsum('gwb,gwc->gbc', vectors, vectors, precision=PRECISE)
    ident = jnp.eye(products.shape[1], dtype=products.dtype)
    factor = jnp.triu(products, 1) + 0.5 * products * ident
    projected = jnp.einsum('gwb,gwc->gbc', vectors, windows, precision=PRECISE)
    coeffs = lax.linalg.triangular_solve(factor, projected, left_side=True, lower=False)
    return windows - jnp.einsum('gwb,gbc->gwc', vectors, coeffs, precision=PRECISE)

def reference(eigvecs, panels, sweep_shift, slot_group):
    all_rows = eigvecs.shape[0]
    all_cols = eigvecs.shape[1]
    positions = jnp.arange(NG, dtype=jnp.int32)
    for sweep_step in range(SWEEPS):
        leading = sweep_step % 2 * B
        rolled = jnp.roll(eigvecs, -leading, axis=0)
        windows = rolled.reshape(NG, 2 * B, all_cols)
        wanted = (positions - sweep_shift[sweep_step]) % NG
        holder = jnp.argsort(slot_group[sweep_step]).astype(jnp.int32)
        slots = holder[wanted.astype(jnp.int32)]
        vectors = panels[sweep_step][slots]
        windows = apply_groups(vectors, windows)
        eigvecs = jnp.roll(windows.reshape(all_rows, all_cols), leading, axis=0)
    return eigvecs
```

```python
import functools

import jax
import jax.numpy as jnp
from jax import lax
from jax.experimental import pallas as pl
from jax.experimental.pallas import tpu as pltpu
from jax.sharding import PartitionSpec as P

F32 = jnp.float32
BF16 = jnp.bfloat16
FULL = lax.Precision.HIGHEST
VMEM_LIMIT = 48 * 1024 * 1024


def dot_full(a, b):
    return jnp.dot(a, b, precision=FULL, preferred_element_type=F32)


def halves(x):
    high = x.astype(BF16)
    low = (x - high.astype(F32)).astype(BF16)
    return high, low


def dot_split(a, b):
    a_high, a_low = a
    b_high, b_low = b
    total = jnp.dot(a_high, b_low, preferred_element_type=F32)
    total += jnp.dot(a_low, b_high, preferred_element_type=F32)
    return total + jnp.dot(a_high, b_high, preferred_element_type=F32)


def inverse_factors(grams):
    order = grams[0].shape[0]
    row = lax.broadcasted_iota(jnp.int32, (order, order), 0)
    col = lax.broadcasted_iota(jnp.int32, (order, order), 1)
    diagonal = row == col

    def corner(width):
        same = (row // (2 * width)) == (col // (2 * width))
        return same & ((row // width) % 2 == 0) & ((col // width) % 2 == 1)

    results = []
    for gram in grams:
        kept = jnp.where(diagonal, gram, 0.0)
        inv_col = 2.0 / jnp.sum(kept, axis=1, keepdims=True)
        inv_row = 2.0 / jnp.sum(kept, axis=0, keepdims=True)
        first = jnp.where(corner(1), gram * inv_col * inv_row, 0.0)
        results.append(jnp.where(diagonal, jnp.broadcast_to(inv_row, gram.shape), 0.0) - first)
    width = 2
    while width < order:
        mask = corner(width)
        inner = [dot_full(x, jnp.where(mask, g, 0.0)) for x, g in zip(results, grams)]
        results = [x - dot_full(i, x) for x, i in zip(results, inner)]
        width *= 2
    return results


def reorder_kernel(shift_ref, group_ref, pieces_ref, out_ref):
    slots, sweeps = pieces_ref.shape[:2]
    cols = out_ref.shape[1]

    def one_slot(slot, carry):
        for sweep in range(sweeps):
            window = lax.rem(group_ref[sweep, slot] + shift_ref[sweep], slots)
            piece = pieces_ref[slot, sweep]
            for c in range(cols):
                out_ref[window, c, sweep] = piece
            if sweep % 2 == 1:
                after = lax.rem(window + 1, slots)
                for c in range(cols):
                    out_ref[after, c, sweeps + sweep // 2] = piece
        return carry

    lax.fori_loop(0, slots, one_slot, 0)


def fetch_panel(recv_ref, block):
    rows, cols, _, piece, band = recv_ref.shape
    parts = [recv_ref[q, c, block] for c in range(cols) for q in range(rows)]
    return jnp.concatenate(parts, axis=0)


def first_kernel(parity_ref, recv_ref, z_ref, core_ref, pair_ref, a_ref):
    half = core_ref.shape[0]
    panel = fetch_panel(recv_ref, 0)
    panel_t = panel.T
    gram = dot_full(panel_t, panel)
    projected = dot_split(halves(panel_t), halves(z_ref[...]))
    (inverse,) = inverse_factors([gram])
    a_ref[...] = dot_full(panel, inverse)
    projected = halves(projected)
    parity = parity_ref[0]
    for out_ref, start in ((core_ref, (1 - parity) * half), (pair_ref, parity * half)):
        rows = pl.ds(pl.multiple_of(start, half), half)
        out_ref[...] = z_ref[rows, :] - dot_split(halves(a_ref[rows, :]), projected)


def arranged(parity, natural):
    before, top, bottom, after = natural
    even = parity == 0
    return [
        jnp.where(even, after, before),
        jnp.where(even, before, after),
        jnp.where(even, bottom, top),
        jnp.where(even, top, bottom),
    ]


def operator_kernel(parity_ref, recv_ref, high1_ref, low1_ref, high2_ref, low2_ref):
    parity = parity_ref[0]
    numbers = (1, 5, 2, 3, 6, 4)
    panels = [fetch_panel(recv_ref, number) for number in numbers]
    panels_t = [p.T for p in panels]
    half = panels[0].shape[0] // 2
    inverses = inverse_factors([dot_full(t, p) for t, p in zip(panels_t, panels)])
    size = 2 * half
    row = lax.broadcasted_iota(jnp.int32, (size, size), 0)
    col = lax.broadcasted_iota(jnp.int32, (size, size), 1)
    identity = jnp.where(row == col, 1.0, 0.0).astype(F32)
    lead = (slice(0, half), slice(half, size), slice(0, size)) * 2
    operators = []
    for panel, panel_t, inverse, rows in zip(panels, panels_t, inverses, lead):
        scaled = dot_full(panel[rows], inverse)
        operators.append(identity[rows] - dot_full(scaled, panel_t))
    for number, high_ref, low_ref in ((0, high1_ref, low1_ref), (3, high2_ref, low2_ref)):
        own, other, last = operators[number : number + 3]
        left = dot_full(last[:, :half], other)
        right = dot_full(last[:, half:], own)
        natural = (left[:, :half], left[:, half:], right[:, :half], right[:, half:])
        merged = jnp.concatenate(arranged(parity, natural), axis=1)
        if number == 0:
            even = parity == 0
            upper, lower = merged[:half], merged[half:]
            merged = jnp.concatenate([jnp.where(even, lower, upper), jnp.where(even, upper, lower)], axis=0)
        high_ref[...], low_ref[...] = halves(merged)


def apply_kernel(high_ref, low_ref, *refs):
    inputs, outputs = refs[:4], refs[4:]
    stacked = jnp.concatenate([ref[...] for ref in inputs], axis=0)
    total = dot_split((high_ref[...], low_ref[...]), halves(stacked))
    at = 0
    for ref in outputs:
        ref[...] = total[at : at + ref.shape[0]]
        at += ref.shape[0]


def call(kernel, in_spaces, outs, scratch=()):
    return pl.pallas_call(
        kernel,
        in_specs=[pl.BlockSpec(memory_space=space) for space in in_spaces],
        out_specs=[pl.BlockSpec(memory_space=pltpu.VMEM) for _ in outs],
        out_shape=[jax.ShapeDtypeStruct(shape, dtype) for shape, dtype in outs],
        scratch_shapes=list(scratch),
        compiler_params=pltpu.CompilerParams(vmem_limit_bytes=VMEM_LIMIT),
    )


def on_device(eigvecs, panels, sweep_shift, slot_group):
    sweeps, _, panel_rows, band = panels.shape
    rows_dev, cols_dev = eigvecs.shape
    half = rows_dev // 2
    row_count, col_count = lax.axis_size("row"), lax.axis_size("col")
    piece = panel_rows // row_count
    smem, vmem = pltpu.SMEM, pltpu.VMEM
    parity = (lax.axis_index("row") % 2).astype(jnp.int32).reshape(1)

    split = panels.reshape(sweeps, row_count, piece, band).transpose(1, 0, 2, 3)
    pieces = lax.all_to_all(split, "row", 0, 0, tiled=True)
    blocks = sweeps + sweeps // 2
    routed_shape = (row_count, col_count, blocks, piece, band)
    (routed,) = call(reorder_kernel, (smem, smem, vmem), [(routed_shape, F32)])(sweep_shift, slot_group, pieces)
    recv = lax.all_to_all(routed.reshape(row_count * col_count, blocks, piece, band), ("row", "col"), 0, 0, tiled=True)
    recv = recv.reshape(routed_shape)

    core_route = [(i, i ^ 1) for i in range(row_count)]
    pair_route = [(i, (i + 1 if i % 2 else i - 1) % row_count) for i in range(row_count)]
    block = ((half, cols_dev), F32)
    own = call(first_kernel, (smem, vmem, vmem), [block, block], [pltpu.VMEM((rows_dev, band), F32)])(parity, recv, eigvecs)
    weight = ((rows_dev, 2 * rows_dev), BF16)
    high1, low1, high2, low2 = call(operator_kernel, (smem, vmem), [weight] * 4)(parity, recv)
    for high, low, outs in ((high1, low1, [block, block]), (high2, low2, [((rows_dev, cols_dev), F32)])):
        from_core = lax.ppermute(own[0], "row", core_route)
        from_pair = lax.ppermute(own[1], "row", pair_route)
        own = call(apply_kernel, (vmem,) * 6, outs)(high, low, from_core, from_pair, *own)
    return own[0]


def solution(mesh):
    in_specs = (P("row", "col"), P(None, "row", "col", None), P(), P())
    return jax.shard_map(on_device, mesh=mesh, in_specs=in_specs, out_specs=P("row", "col"), check_vma=False)
```

```python
import functools

import jax
import jax.numpy as jnp
from jax import lax
from jax.experimental import pallas as pl
from jax.experimental.pallas import tpu as pltpu
from jax.sharding import PartitionSpec as P

F32 = jnp.float32
BF16 = jnp.bfloat16
VMEM_LIMIT = 48 * 1024 * 1024


def mxu(a, b):
    return jnp.dot(a, b, preferred_element_type=F32)


def beside(*blocks):
    return jnp.concatenate(blocks, axis=1)


def above(*blocks):
    return jnp.concatenate(blocks, axis=0)


def halves(x):
    high = x.astype(BF16)
    low = (x - high.astype(F32)).astype(BF16)
    return high, low


def thirds(x):
    high = x.astype(BF16)
    rest = x - high.astype(F32)
    middle = rest.astype(BF16)
    return high, middle, (rest - middle.astype(F32)).astype(BF16)


def dot_full(a, b):
    a_high, a_middle, a_low = thirds(a)
    b_high, b_middle, b_low = thirds(b)
    depth, width = b.shape
    small = mxu(beside(a_high, a_low), above(b_low, b_high))
    if depth > 128:
        large = mxu(a_high, beside(b_high, b_middle))
        large += mxu(a_middle, beside(b_high, b_middle))
    elif width > 128:
        left = beside(a_high, a_middle)
        return small + mxu(left, above(b_middle, b_middle)) + mxu(left, above(b_high, b_high))
    else:
        right = beside(b_high, b_middle)
        large = mxu(beside(a_high, a_middle), above(right, right))
    return small + large[:, width:] + large[:, :width]


def dot_split(a, b):
    a_high, a_low = a
    b_high, b_low = b
    if b_high.shape[0] > 128:
        return mxu(a_high, b_low) + mxu(a_low, b_high) + mxu(a_high, b_high)
    return mxu(a_high, b_low) + mxu(beside(a_high, a_low), above(b_high, b_high))


def inverse_factors(grams):
    order = grams[0].shape[0]
    row = lax.broadcasted_iota(jnp.int32, (order, order), 0)
    col = lax.broadcasted_iota(jnp.int32, (order, order), 1)
    diagonal = row == col

    def corner(width):
        same = (row // (2 * width)) == (col // (2 * width))
        return same & ((row // width) % 2 == 0) & ((col // width) % 2 == 1)

    results = []
    for gram in grams:
        kept = jnp.where(diagonal, gram, 0.0)
        inv_col = 2.0 / jnp.sum(kept, axis=1, keepdims=True)
        inv_row = 2.0 / jnp.sum(kept, axis=0, keepdims=True)
        first = jnp.where(corner(1), gram * inv_col * inv_row, 0.0)
        results.append(jnp.where(diagonal, jnp.broadcast_to(inv_row, gram.shape), 0.0) - first)
    width = 2
    while width < order:
        if 4 * width <= order:
            mask = ((row // (4 * width)) == (col // (4 * width))) & ((row // width) < (col // width))
            inner = [dot_full(x, jnp.where(mask, g, 0.0)) for x, g in zip(results, grams)]
            squares = [dot_full(n, n) for n in inner]
            once = [x - dot_full(n, x) for x, n in zip(results, inner)]
            results = [y + dot_full(n, y) for y, n in zip(once, squares)]
            width *= 4
        else:
            mask = corner(width)
            inner = [dot_full(x, jnp.where(mask, g, 0.0)) for x, g in zip(results, grams)]
            results = [x - dot_full(n, x) for x, n in zip(results, inner)]
            width *= 2
    return results


def wrapped(index, size):
    return jnp.where(index >= size, index - size, index)


def reorder_kernel(layout, shift_ref, group_ref, pieces_ref, out_ref, buffer, sem):
    slots = pieces_ref.shape[0]
    for slot in range(slots):
        for sweep, targets in enumerate(layout):
            window = wrapped(group_ref[sweep, slot] + shift_ref[sweep], slots)
            piece = pieces_ref[slot, sweep]
            for block, columns, distance in targets:
                target = wrapped(window + 1, slots) if distance else window
                for c in columns:
                    buffer[target, c, block] = piece
    copy = pltpu.make_async_copy(buffer, out_ref, sem)
    copy.start()
    copy.wait()


def fetch_panel(recv_ref, *index):
    rows, cols = recv_ref.shape[:2]
    parts = [recv_ref[(q, c) + index] for c in range(cols) for q in range(rows)]
    return jnp.concatenate(parts, axis=0)


def first_kernel(groups, place_ref, recv_ref, z_ref, core_ref, pair_ref, *refs):
    half = core_ref.shape[0]
    a_ref, sem = refs[-2:]
    copies = []
    for blocks, ref in zip(groups, refs[:-2]):
        for number, block in enumerate(blocks):
            copies.append(pltpu.make_async_copy(recv_ref.at[:, :, block], ref.at[:, :, number], sem.at[len(copies)]))
            copies[-1].start()
    panel = fetch_panel(recv_ref, 0)
    panel_t = panel.T
    gram = dot_full(panel_t, panel)
    projected = halves(dot_split(halves(panel_t), halves(z_ref[...])))
    (inverse,) = inverse_factors([gram])
    a_ref[...] = dot_full(panel, inverse)
    parity = place_ref[0]
    for out_ref, start in ((core_ref, (1 - parity) * half), (pair_ref, parity * half)):
        rows = pl.ds(pl.multiple_of(start, half), half)
        out_ref[...] = z_ref[rows, :] - dot_split(halves(a_ref[rows, :]), projected)
    for copy in copies:
        copy.wait()


def arranged(parity, natural):
    before, top, bottom, after = natural
    even = parity == 0
    return [
        jnp.where(even, before, after),
        jnp.where(even, after, before),
        jnp.where(even, bottom, top),
        jnp.where(even, top, bottom),
    ]


def operator_kernel(odd, even, for_exchange, place_ref, *refs):
    sources, (core_in, core_own, pair_own, partial_ref, high_ref, low_ref) = refs[:-6], refs[-6:]
    parity, column = place_ref[0], place_ref[1]

    def panel_of(choices):
        chosen = [fetch_panel(sources[source], block) for source, block in choices]
        return chosen[0] if len(chosen) == 1 else jnp.where(column == 0, chosen[0], chosen[1])

    panels = [panel_of(choices) for choices in (*odd, even)]
    panels_t = [p.T for p in panels]
    size = panels[0].shape[0]
    half = size // 2
    inverses = inverse_factors([dot_full(t, p) for t, p in zip(panels_t, panels)])
    row = lax.broadcasted_iota(jnp.int32, (size, size), 0)
    col = lax.broadcasted_iota(jnp.int32, (size, size), 1)
    identity = jnp.where(row == col, 1.0, 0.0).astype(F32)
    operators = []
    for panel, panel_t, inverse, rows in zip(panels, panels_t, inverses, (slice(0, half), slice(half, size), slice(0, size))):
        scaled = dot_full(panel[rows], inverse)
        operators.append(identity[rows] - dot_full(scaled, panel_t))
    own, other, last = operators
    if for_exchange:
        flipped = parity == 0
        upper, lower = last[:half], last[half:]
        last = jnp.concatenate([jnp.where(flipped, lower, upper), jnp.where(flipped, upper, lower)], axis=0)
    left = dot_split(halves(last[:, :half]), halves(other))
    right = dot_split(halves(last[:, half:]), halves(own))
    natural = (left[:, :half], left[:, half:], right[:, :half], right[:, half:])
    first, *rest = arranged(parity, natural)
    high_ref[...], low_ref[...] = halves(first)
    rows = jnp.concatenate([core_in[...], core_own[...], pair_own[...]], axis=0)
    partial_ref[...] = dot_split(halves(jnp.concatenate(rest, axis=1)), halves(rows))


def apply_kernel(high_ref, low_ref, pair_in, partial_ref, *outputs):
    total = dot_split((high_ref[...], low_ref[...]), halves(pair_in[...])) + partial_ref[...]
    at = 0
    for ref in outputs:
        ref[...] = total[at : at + ref.shape[0]]
        at += ref.shape[0]


def last_kernel(high_ref, low_ref, pair_in, partial_ref, out_ref, result, sems):
    columns = pair_in.shape[1]
    chunk = columns // sems.shape[0]
    copies = []
    for number in range(sems.shape[0]):
        at = pl.ds(number * chunk, chunk)
        result[:, at] = dot_split((high_ref[...], low_ref[...]), halves(pair_in[:, at])) + partial_ref[:, at]
        copies.append(pltpu.make_async_copy(result.at[:, at], out_ref.at[:, at], sems.at[number]))
        copies[-1].start()
    for copy in copies:
        copy.wait()


def call(kernel, in_spaces, outs, scratch=(), out_space=pltpu.VMEM):
    return pl.pallas_call(
        kernel,
        in_specs=[pl.BlockSpec(memory_space=space) for space in in_spaces],
        out_specs=[pl.BlockSpec(memory_space=out_space) for _ in outs],
        out_shape=[jax.ShapeDtypeStruct(shape, dtype) for shape, dtype in outs],
        scratch_shapes=list(scratch),
        compiler_params=pltpu.CompilerParams(vmem_limit_bytes=VMEM_LIMIT),
    )


def on_device(eigvecs, panels, sweep_shift, slot_group):
    sweeps, _, panel_rows, band = panels.shape
    rows_dev, cols_dev = eigvecs.shape
    half = rows_dev // 2
    row_count, col_count = lax.axis_size("row"), lax.axis_size("col")
    piece = panel_rows // row_count
    smem, vmem = pltpu.SMEM, pltpu.VMEM
    place = jnp.stack([lax.axis_index("row") % 2, lax.axis_index("col")]).astype(jnp.int32)

    core_route = [(i, i ^ 1) for i in range(row_count)]
    pair_route = [(i, (i + 1 if i % 2 else i - 1) % row_count) for i in range(row_count)]

    split = panels.reshape(sweeps, row_count, piece, band).transpose(1, 0, 2, 3)
    pieces = lax.all_to_all(split, "row", 0, 0, tiled=True)
    columns = tuple(range(col_count))
    paired = col_count == 2
    if paired:
        one, two = (0,), (1,)
        layout = (
            ((0, columns, 0),),
            ((1, one, 0), (1, two, 1)),
            ((2, one, 0),),
            ((3, one, 0), (3, two, 1)),
            ((2, two, 0),),
        )
        groups = ((1, 2), (3,))
    else:
        layout = (
            ((0, columns, 0),),
            ((1, columns, 0), (2, columns, 1)),
            ((3, columns, 0),),
            ((4, columns, 0), (5, columns, 1)),
            ((6, columns, 0),),
        )
        groups = ()
    blocks = 1 + max(target[0] for targets in layout for target in targets)
    shape = (row_count, col_count, blocks, piece, band)
    (routed,) = call(
        functools.partial(reorder_kernel, layout),
        (smem, smem, vmem),
        [(shape, F32)],
        [vmem(shape, F32), pltpu.SemaphoreType.DMA(())],
        pltpu.HBM,
    )(sweep_shift, slot_group, pieces)
    flat = routed.reshape((row_count * col_count, blocks, piece, band))
    recv = lax.all_to_all(flat, ("row", "col"), 0, 0, tiled=True).reshape(shape)

    block = ((half, cols_dev), F32)
    whole = ((rows_dev, cols_dev), F32)
    handed = [((row_count, col_count, len(group), piece, band), F32) for group in groups]
    scratch = [vmem((rows_dev, band), F32), pltpu.SemaphoreType.DMA((3,))]
    kernel = functools.partial(first_kernel, groups)
    for_core, for_pair, *here = call(kernel, (smem, vmem, vmem), [block, block, *handed], scratch)(place, recv, eigvecs)

    def operators(number, for_exchange, from_core, for_core, for_pair):
        if paired:
            sources = (here[0], there[0]) if number == 0 else (here[0], there[0], here[1], there[1])
            if number == 0:
                odd, even = (((0, 0), (1, 0)), ((1, 0), (0, 0))), ((0, 1), (1, 1))
            else:
                odd, even = (((2, 0), (3, 0)), ((3, 0), (2, 0))), ((1, 1), (0, 1))
        else:
            sources = (recv,)
            odd, even = (((0, 1 + 3 * number),), ((0, 2 + 3 * number),)), ((0, 3 + 3 * number),)
        kernel = functools.partial(operator_kernel, odd, even, for_exchange)
        weight = ((rows_dev, half), BF16)
        inputs = (place, *sources, from_core, for_core, for_pair)
        return call(kernel, (smem,) + (vmem,) * (len(inputs) - 1), [whole, weight, weight])(*inputs)

    from_pair = lax.ppermute(for_pair, "row", pair_route)
    from_core = lax.ppermute(for_core, "row", core_route)
    there = [lax.ppermute(tiles, "col", [(0, 1), (1, 0)]) for tiles in here]
    partial, high, low = operators(0, True, from_core, for_core, for_pair)
    for_core, for_pair = call(apply_kernel, (vmem,) * 4, [block] * 2)(high, low, from_pair, partial)
    from_pair = lax.ppermute(for_pair, "row", pair_route)
    from_core = lax.ppermute(for_core, "row", core_route)
    partial, high, low = operators(1, False, from_core, for_core, for_pair)
    chunks = [vmem(*whole), pltpu.SemaphoreType.DMA((4 if cols_dev % 512 == 0 else 1,))]
    return call(last_kernel, (vmem,) * 4, [whole], chunks, pl.ANY)(high, low, from_pair, partial)[0]


def solution(mesh):
    in_specs = (P("row", "col"), P(None, "row", "col", None), P(), P())
    return jax.shard_map(on_device, mesh=mesh, in_specs=in_specs, out_specs=P("row", "col"), check_vma=False)
```

```python
import functools

import jax
import jax.numpy as jnp
from jax import lax
from jax.experimental import pallas as pl
from jax.experimental.pallas import tpu as pltpu
from jax.sharding import PartitionSpec as P

F32 = jnp.float32
BF16 = jnp.bfloat16
VMEM_LIMIT = 48 * 1024 * 1024


def mxu(a, b):
    return jnp.dot(a, b, preferred_element_type=F32)


def beside(*blocks):
    return jnp.concatenate(blocks, axis=1)


def above(*blocks):
    return jnp.concatenate(blocks, axis=0)


def halves(x):
    high = x.astype(BF16)
    low = (x - high.astype(F32)).astype(BF16)
    return high, low


def thirds(x):
    high = x.astype(BF16)
    rest = x - high.astype(F32)
    middle = rest.astype(BF16)
    return high, middle, (rest - middle.astype(F32)).astype(BF16)


def dot_full(a, b):
    a_high, a_middle, a_low = thirds(a)
    b_high, b_middle, b_low = thirds(b)
    depth, width = b.shape
    small = mxu(beside(a_high, a_low), above(b_low, b_high))
    if depth > 128:
        large = mxu(a_high, beside(b_high, b_middle))
        large += mxu(a_middle, beside(b_high, b_middle))
    elif width > 128:
        left = beside(a_high, a_middle)
        return small + mxu(left, above(b_middle, b_middle)) + mxu(left, above(b_high, b_high))
    else:
        right = beside(b_high, b_middle)
        large = mxu(beside(a_high, a_middle), above(right, right))
    return small + large[:, width:] + large[:, :width]


def dot_split(a, b):
    a_high, a_low = a
    b_high, b_low = b
    if b_high.shape[0] > 128:
        return mxu(a_high, b_low) + mxu(a_low, b_high) + mxu(a_high, b_high)
    return mxu(a_high, b_low) + mxu(beside(a_high, a_low), above(b_high, b_high))


def inverse_factors(grams):
    order = grams[0].shape[0]
    row = lax.broadcasted_iota(jnp.int32, (order, order), 0)
    col = lax.broadcasted_iota(jnp.int32, (order, order), 1)
    diagonal = row == col

    def corner(width):
        same = (row // (2 * width)) == (col // (2 * width))
        return same & ((row // width) % 2 == 0) & ((col // width) % 2 == 1)

    results = []
    for gram in grams:
        kept = jnp.where(diagonal, gram, 0.0)
        inv_col = 2.0 / jnp.sum(kept, axis=1, keepdims=True)
        inv_row = 2.0 / jnp.sum(kept, axis=0, keepdims=True)
        first = jnp.where(corner(1), gram * inv_col * inv_row, 0.0)
        results.append(jnp.where(diagonal, jnp.broadcast_to(inv_row, gram.shape), 0.0) - first)
    width = 2
    while width < order:
        if 4 * width <= order:
            mask = ((row // (4 * width)) == (col // (4 * width))) & ((row // width) < (col // width))
            inner = [dot_full(x, jnp.where(mask, g, 0.0)) for x, g in zip(results, grams)]
            squares = [dot_full(n, n) for n in inner]
            once = [x - dot_full(n, x) for x, n in zip(results, inner)]
            results = [y + dot_full(n, y) for y, n in zip(once, squares)]
            width *= 4
        else:
            mask = corner(width)
            inner = [dot_full(x, jnp.where(mask, g, 0.0)) for x, g in zip(results, grams)]
            results = [x - dot_full(n, x) for x, n in zip(results, inner)]
            width *= 2
    return results


def wrapped(index, size):
    return jnp.where(index >= size, index - size, index)


def reorder_kernel(layout, shift_ref, group_ref, pieces_ref, out_ref):
    slots = pieces_ref.shape[0]
    for slot in range(slots):
        for sweep, targets in enumerate(layout):
            window = wrapped(group_ref[sweep, slot] + shift_ref[sweep], slots)
            piece = pieces_ref[slot, sweep]
            for block, columns, distance in targets:
                target = wrapped(window + 1, slots) if distance else window
                for c in columns:
                    out_ref[target, c, block] = piece


def fetch_panel(recv_ref, *index):
    rows, cols = recv_ref.shape[:2]
    parts = [recv_ref[(q, c) + index] for c in range(cols) for q in range(rows)]
    return jnp.concatenate(parts, axis=0)


def first_kernel(groups, place_ref, recv_ref, z_ref, core_ref, pair_ref, *refs):
    half = core_ref.shape[0]
    a_ref, sem = refs[-2:]
    copies = []
    for blocks, ref in zip(groups, refs[:-2]):
        for number, block in enumerate(blocks):
            copies.append(pltpu.make_async_copy(recv_ref.at[:, :, block], ref.at[:, :, number], sem.at[len(copies)]))
            copies[-1].start()
    panel = fetch_panel(recv_ref, 0)
    panel_t = panel.T
    gram = dot_full(panel_t, panel)
    projected = halves(dot_split(halves(panel_t), halves(z_ref[...])))
    (inverse,) = inverse_factors([gram])
    a_ref[...] = dot_full(panel, inverse)
    parity = place_ref[0]
    for out_ref, start in ((core_ref, (1 - parity) * half), (pair_ref, parity * half)):
        rows = pl.ds(pl.multiple_of(start, half), half)
        out_ref[...] = z_ref[rows, :] - dot_split(halves(a_ref[rows, :]), projected)
    for copy in copies:
        copy.wait()


def arranged(parity, natural):
    before, top, bottom, after = natural
    even = parity == 0
    return [
        jnp.where(even, before, after),
        jnp.where(even, after, before),
        jnp.where(even, bottom, top),
        jnp.where(even, top, bottom),
    ]


def operator_kernel(odd, even, for_exchange, place_ref, *refs):
    sources, (core_own, pair_own, partial_ref, high_ref, low_ref) = refs[:-5], refs[-5:]
    parity, column = place_ref[0], place_ref[1]

    def panel_of(choices):
        chosen = [fetch_panel(sources[source], block) for source, block in choices]
        return chosen[0] if len(chosen) == 1 else jnp.where(column == 0, chosen[0], chosen[1])

    panels = [panel_of(choices) for choices in (*odd, even)]
    panels_t = [p.T for p in panels]
    size = panels[0].shape[0]
    half = size // 2
    inverses = inverse_factors([dot_full(t, p) for t, p in zip(panels_t, panels)])
    row = lax.broadcasted_iota(jnp.int32, (size, size), 0)
    col = lax.broadcasted_iota(jnp.int32, (size, size), 1)
    identity = jnp.where(row == col, 1.0, 0.0).astype(F32)
    operators = []
    for panel, panel_t, inverse, rows in zip(panels, panels_t, inverses, (slice(0, half), slice(half, size), slice(0, size))):
        scaled = dot_full(panel[rows], inverse)
        operators.append(identity[rows] - dot_full(scaled, panel_t))
    own, other, last = operators
    if for_exchange:
        flipped = parity == 0
        upper, lower = last[:half], last[half:]
        last = jnp.concatenate([jnp.where(flipped, lower, upper), jnp.where(flipped, upper, lower)], axis=0)
    left = dot_split(halves(last[:, :half]), halves(other))
    right = dot_split(halves(last[:, half:]), halves(own))
    natural = (left[:, :half], left[:, half:], right[:, :half], right[:, half:])
    pair_columns, core_columns, *rest = arranged(parity, natural)
    high_ref[...], low_ref[...] = halves(beside(pair_columns, core_columns))
    partial_ref[...] = dot_split(halves(beside(*rest)), halves(above(core_own[...], pair_own[...])))


def apply_kernel(high_ref, low_ref, pair_in, core_in, partial_ref, *outputs):
    total = dot_split((high_ref[...], low_ref[...]), halves(above(pair_in[...], core_in[...]))) + partial_ref[...]
    at = 0
    for ref in outputs:
        ref[...] = total[at : at + ref.shape[0]]
        at += ref.shape[0]


def last_kernel(high_ref, low_ref, pair_in, core_in, partial_ref, out_ref, result, sems):
    columns = pair_in.shape[1]
    chunk = columns // sems.shape[0]
    copies = []
    for number in range(sems.shape[0]):
        at = pl.ds(number * chunk, chunk)
        far = halves(above(pair_in[:, at], core_in[:, at]))
        result[:, at] = dot_split((high_ref[...], low_ref[...]), far) + partial_ref[:, at]
        copies.append(pltpu.make_async_copy(result.at[:, at], out_ref.at[:, at], sems.at[number]))
        copies[-1].start()
    for copy in copies:
        copy.wait()


def call(kernel, in_spaces, outs, scratch=(), out_space=pltpu.VMEM):
    return pl.pallas_call(
        kernel,
        in_specs=[pl.BlockSpec(memory_space=space) for space in in_spaces],
        out_specs=[pl.BlockSpec(memory_space=out_space) for _ in outs],
        out_shape=[jax.ShapeDtypeStruct(shape, dtype) for shape, dtype in outs],
        scratch_shapes=list(scratch),
        compiler_params=pltpu.CompilerParams(vmem_limit_bytes=VMEM_LIMIT),
    )


def on_device(eigvecs, panels, sweep_shift, slot_group):
    sweeps, _, panel_rows, band = panels.shape
    rows_dev, cols_dev = eigvecs.shape
    half = rows_dev // 2
    row_count, col_count = lax.axis_size("row"), lax.axis_size("col")
    piece = panel_rows // row_count
    smem, vmem = pltpu.SMEM, pltpu.VMEM
    place = jnp.stack([lax.axis_index("row") % 2, lax.axis_index("col")]).astype(jnp.int32)

    core_route = [(i, i ^ 1) for i in range(row_count)]
    pair_route = [(i, (i + 1 if i % 2 else i - 1) % row_count) for i in range(row_count)]

    panels, place = lax.optimization_barrier((panels, place))
    split = panels.reshape(sweeps, row_count, piece, band).transpose(1, 0, 2, 3)
    pieces = lax.all_to_all(split, "row", 0, 0, tiled=True)
    columns = tuple(range(col_count))
    paired = col_count == 2
    if paired:
        one, two = (0,), (1,)
        layout = (
            ((0, columns, 0),),
            ((1, one, 0), (1, two, 1)),
            ((2, one, 0),),
            ((3, one, 0), (3, two, 1)),
            ((2, two, 0),),
        )
        groups = ((1, 2), (3,))
    else:
        layout = (
            ((0, columns, 0),),
            ((1, columns, 0), (2, columns, 1)),
            ((3, columns, 0),),
            ((4, columns, 0), (5, columns, 1)),
            ((6, columns, 0),),
        )
        groups = ()
    blocks = 1 + max(target[0] for targets in layout for target in targets)
    shape = (row_count, col_count, blocks, piece, band)
    (routed,) = call(
        functools.partial(reorder_kernel, layout),
        (smem, smem, vmem),
        [(shape, F32)],
    )(sweep_shift, slot_group, pieces)
    flat = routed.reshape((row_count * col_count, blocks, piece, band))
    recv = lax.all_to_all(flat, ("row", "col"), 0, 0, tiled=True).reshape(shape)

    block = ((half, cols_dev), F32)
    whole = ((rows_dev, cols_dev), F32)
    handed = [((row_count, col_count, len(group), piece, band), F32) for group in groups]
    scratch = [vmem((rows_dev, band), F32), pltpu.SemaphoreType.DMA((3,))]
    kernel = functools.partial(first_kernel, groups)
    for_core, for_pair, *here = call(kernel, (smem, vmem, vmem), [block, block, *handed], scratch)(place, recv, eigvecs)

    def operators(number, for_exchange, for_core, for_pair):
        if paired:
            sources = (here[0], there[0]) if number == 0 else (here[0], there[0], here[1], there[1])
            if number == 0:
                odd, even = (((0, 0), (1, 0)), ((1, 0), (0, 0))), ((0, 1), (1, 1))
            else:
                odd, even = (((2, 0), (3, 0)), ((3, 0), (2, 0))), ((1, 1), (0, 1))
        else:
            sources = (recv,)
            odd, even = (((0, 1 + 3 * number),), ((0, 2 + 3 * number),)), ((0, 3 + 3 * number),)
        kernel = functools.partial(operator_kernel, odd, even, for_exchange)
        weight = ((rows_dev, rows_dev), BF16)
        inputs = (place, *sources, for_core, for_pair)
        return call(kernel, (smem,) + (vmem,) * (len(inputs) - 1), [whole, weight, weight])(*inputs)

    def exchange(number, for_core, for_pair):
        from_pair = lax.ppermute(for_pair, "row", pair_route)
        if paired:
            there.append(lax.ppermute(here[number], "col", [(0, 1), (1, 0)]))
            for_core, there[number] = lax.optimization_barrier((for_core, there[number]))
        return from_pair, lax.ppermute(for_core, "row", core_route)

    there = []
    received = exchange(0, for_core, for_pair)
    partial, high, low = operators(0, True, for_core, for_pair)
    for_core, for_pair = call(apply_kernel, (vmem,) * 5, [block] * 2)(high, low, *received, partial)
    received = exchange(1, for_core, for_pair)
    partial, high, low = operators(1, False, for_core, for_pair)
    chunks = [vmem(*whole), pltpu.SemaphoreType.DMA((4 if cols_dev % 512 == 0 else 1,))]
    return call(last_kernel, (vmem,) * 5, [whole], chunks, pl.ANY)(high, low, *received, partial)[0]


def solution(mesh):
    in_specs = (P("row", "col"), P(None, "row", "col", None), P(), P())
    return jax.shard_map(on_device, mesh=mesh, in_specs=in_specs, out_specs=P("row", "col"), check_vma=False)
```

```python
import functools

import jax
import jax.numpy as jnp
from jax import lax
from jax.experimental import pallas as pl
from jax.experimental.pallas import tpu as pltpu
from jax.sharding import PartitionSpec as P

F32 = jnp.float32
BF16 = jnp.bfloat16
VMEM_LIMIT = 48 * 1024 * 1024
OUT_CHUNKS = 2


def mxu(a, b):
    return jnp.dot(a, b, preferred_element_type=F32)


def beside(*blocks):
    return jnp.concatenate(blocks, axis=1)


def above(*blocks):
    return jnp.concatenate(blocks, axis=0)


def halves(x):
    high = x.astype(BF16)
    low = (x - high.astype(F32)).astype(BF16)
    return high, low


def thirds(x):
    high = x.astype(BF16)
    rest = x - high.astype(F32)
    middle = rest.astype(BF16)
    return high, middle, (rest - middle.astype(F32)).astype(BF16)


def dot_full(a, b):
    a_high, a_middle, a_low = thirds(a)
    b_high, b_middle, b_low = thirds(b)
    depth, width = b.shape
    small = mxu(beside(a_high, a_low), above(b_low, b_high))
    if depth > 128:
        large = mxu(a_high, beside(b_high, b_middle))
        large += mxu(a_middle, beside(b_high, b_middle))
    elif width > 128:
        left = beside(a_high, a_middle)
        return small + mxu(left, above(b_middle, b_middle)) + mxu(left, above(b_high, b_high))
    else:
        right = beside(b_high, b_middle)
        large = mxu(beside(a_high, a_middle), above(right, right))
    return small + large[:, width:] + large[:, :width]


def dot_split(a, b):
    a_high, a_low = a
    b_high, b_low = b
    if b_high.shape[0] > 128:
        return mxu(a_high, b_low) + mxu(a_low, b_high) + mxu(a_high, b_high)
    return mxu(a_high, b_low) + mxu(beside(a_high, a_low), above(b_high, b_high))


def inverse_factors(grams):
    order = grams[0].shape[0]
    row = lax.broadcasted_iota(jnp.int32, (order, order), 0)
    col = lax.broadcasted_iota(jnp.int32, (order, order), 1)
    diagonal = row == col

    def corner(width):
        same = (row // (2 * width)) == (col // (2 * width))
        return same & ((row // width) % 2 == 0) & ((col // width) % 2 == 1)

    results = []
    for gram in grams:
        kept = jnp.where(diagonal, gram, 0.0)
        inv_col = 2.0 / jnp.sum(kept, axis=1, keepdims=True)
        inv_row = 2.0 / jnp.sum(kept, axis=0, keepdims=True)
        first = jnp.where(corner(1), gram * inv_col * inv_row, 0.0)
        results.append(jnp.where(diagonal, jnp.broadcast_to(inv_row, gram.shape), 0.0) - first)
    width = 2
    while width < order:
        if 4 * width <= order:
            mask = ((row // (4 * width)) == (col // (4 * width))) & ((row // width) < (col // width))
            inner = [dot_full(x, jnp.where(mask, g, 0.0)) for x, g in zip(results, grams)]
            squares = [dot_full(n, n) for n in inner]
            once = [x - dot_full(n, x) for x, n in zip(results, inner)]
            results = [y + dot_full(n, y) for y, n in zip(once, squares)]
            width *= 4
        else:
            mask = corner(width)
            inner = [dot_full(x, jnp.where(mask, g, 0.0)) for x, g in zip(results, grams)]
            results = [x - dot_full(n, x) for x, n in zip(results, inner)]
            width *= 2
    return results


def wrapped(index, size):
    return jnp.where(index >= size, index - size, index)


def reorder_kernel(layout, shift_ref, group_ref, pieces_ref, out_ref):
    slots = pieces_ref.shape[0]
    for slot in range(slots):
        for sweep, targets in enumerate(layout):
            window = wrapped(group_ref[sweep, slot] + shift_ref[sweep], slots)
            piece = pieces_ref[slot, sweep]
            for block, columns, distance in targets:
                target = wrapped(window + 1, slots) if distance else window
                for c in columns:
                    out_ref[target, c, block] = piece


def fetch_panel(recv_ref, *index):
    rows, cols = recv_ref.shape[:2]
    parts = [recv_ref[(q, c) + index] for c in range(cols) for q in range(rows)]
    return jnp.concatenate(parts, axis=0)


def first_kernel(groups, place_ref, recv_ref, z_ref, core_ref, pair_ref, *refs):
    half = core_ref.shape[0]
    a_ref, sem = refs[-2:]
    copies = []
    for blocks, ref in zip(groups, refs[:-2]):
        for number, block in enumerate(blocks):
            copies.append(pltpu.make_async_copy(recv_ref.at[:, :, block], ref.at[:, :, number], sem.at[len(copies)]))
            copies[-1].start()
    panel = fetch_panel(recv_ref, 0)
    panel_t = panel.T
    gram = dot_full(panel_t, panel)
    projected = halves(dot_split(halves(panel_t), halves(z_ref[...])))
    (inverse,) = inverse_factors([gram])
    a_ref[...] = dot_full(panel, inverse)
    parity = place_ref[0]
    for out_ref, start in ((core_ref, (1 - parity) * half), (pair_ref, parity * half)):
        rows = pl.ds(pl.multiple_of(start, half), half)
        out_ref[...] = z_ref[rows, :] - dot_split(halves(a_ref[rows, :]), projected)
    for copy in copies:
        copy.wait()


def arranged(parity, natural):
    before, top, bottom, after = natural
    even = parity == 0
    return [
        jnp.where(even, before, after),
        jnp.where(even, after, before),
        jnp.where(even, bottom, top),
        jnp.where(even, top, bottom),
    ]


def operator_kernel(odd, even, for_exchange, known, place_ref, *refs):
    partial_ref, high_ref, low_ref = refs[-3:]
    sources, inputs = refs[: -3 - known], refs[-3 - known : -3]
    parity, column = place_ref[0], place_ref[1]

    def panel_of(choices):
        chosen = [fetch_panel(sources[source], block) for source, block in choices]
        return chosen[0] if len(chosen) == 1 else jnp.where(column == 0, chosen[0], chosen[1])

    panels = [panel_of(choices) for choices in (*odd, even)]
    panels_t = [p.T for p in panels]
    size = panels[0].shape[0]
    half = size // 2
    inverses = inverse_factors([dot_full(t, p) for t, p in zip(panels_t, panels)])
    row = lax.broadcasted_iota(jnp.int32, (size, size), 0)
    col = lax.broadcasted_iota(jnp.int32, (size, size), 1)
    identity = jnp.where(row == col, 1.0, 0.0).astype(F32)
    operators = []
    for panel, panel_t, inverse, rows in zip(panels, panels_t, inverses, (slice(0, half), slice(half, size), slice(0, size))):
        scaled = dot_full(panel[rows], inverse)
        operators.append(identity[rows] - dot_full(scaled, panel_t))
    own, other, last = operators
    if for_exchange:
        flipped = parity == 0
        upper, lower = last[:half], last[half:]
        last = jnp.concatenate([jnp.where(flipped, lower, upper), jnp.where(flipped, upper, lower)], axis=0)
    left = dot_split(halves(last[:, :half]), halves(other))
    right = dot_split(halves(last[:, half:]), halves(own))
    natural = (left[:, :half], left[:, half:], right[:, :half], right[:, half:])
    order = arranged(parity, natural)
    high_ref[...], low_ref[...] = halves(beside(*order[: 4 - known]))
    rows = above(*(ref[...] for ref in inputs))
    partial_ref[...] = dot_split(halves(beside(*order[4 - known :])), halves(rows))


def apply_kernel(high_ref, low_ref, pair_in, core_in, partial_ref, core_out, pair_out):
    half = core_out.shape[0]
    total = dot_split((high_ref[...], low_ref[...]), halves(above(pair_in[...], core_in[...]))) + partial_ref[...]
    core_out[...] = total[:half]
    pair_out[...] = total[half:]


def last_kernel(high_ref, low_ref, pair_in, partial_ref, out_ref, result, sems):
    chunk = pair_in.shape[1] // sems.shape[0]
    copies = []
    for number in range(sems.shape[0]):
        at = pl.ds(number * chunk, chunk)
        result[:, at] = dot_split((high_ref[...], low_ref[...]), halves(pair_in[:, at])) + partial_ref[:, at]
        copies.append(pltpu.make_async_copy(result.at[:, at], out_ref.at[:, at], sems.at[number]))
        copies[-1].start()
    for copy in copies:
        copy.wait()


def call(kernel, in_spaces, outs, scratch=(), out_space=pltpu.VMEM):
    return pl.pallas_call(
        kernel,
        in_specs=[pl.BlockSpec(memory_space=space) for space in in_spaces],
        out_specs=[pl.BlockSpec(memory_space=out_space) for _ in outs],
        out_shape=[jax.ShapeDtypeStruct(shape, dtype) for shape, dtype in outs],
        scratch_shapes=list(scratch),
        compiler_params=pltpu.CompilerParams(vmem_limit_bytes=VMEM_LIMIT),
    )


def on_device(eigvecs, panels, sweep_shift, slot_group):
    sweeps, _, panel_rows, band = panels.shape
    rows_dev, cols_dev = eigvecs.shape
    half = rows_dev // 2
    row_count, col_count = lax.axis_size("row"), lax.axis_size("col")
    piece = panel_rows // row_count
    smem, vmem = pltpu.SMEM, pltpu.VMEM
    place = jnp.stack([lax.axis_index("row") % 2, lax.axis_index("col")]).astype(jnp.int32)

    core_route = [(i, i ^ 1) for i in range(row_count)]
    pair_route = [(i, (i + 1 if i % 2 else i - 1) % row_count) for i in range(row_count)]

    panels, place = lax.optimization_barrier((panels, place))
    split = panels.reshape(sweeps, row_count, piece, band).transpose(1, 0, 2, 3)
    pieces = lax.all_to_all(split, "row", 0, 0, tiled=True)
    columns = tuple(range(col_count))
    paired = col_count == 2
    if paired:
        one, two = (0,), (1,)
        layout = (
            ((0, columns, 0),),
            ((1, one, 0), (1, two, 1)),
            ((2, one, 0),),
            ((3, one, 0), (3, two, 1)),
            ((2, two, 0),),
        )
        groups = ((1, 2), (3,))
    else:
        layout = (
            ((0, columns, 0),),
            ((1, columns, 0), (2, columns, 1)),
            ((3, columns, 0),),
            ((4, columns, 0), (5, columns, 1)),
            ((6, columns, 0),),
        )
        groups = ()
    blocks = 1 + max(target[0] for targets in layout for target in targets)
    shape = (row_count, col_count, blocks, piece, band)
    (routed,) = call(
        functools.partial(reorder_kernel, layout),
        (smem, smem, vmem),
        [(shape, F32)],
    )(sweep_shift, slot_group, pieces)
    flat = routed.reshape((row_count * col_count, blocks, piece, band))
    recv = lax.all_to_all(flat, ("row", "col"), 0, 0, tiled=True).reshape(shape)

    block = ((half, cols_dev), F32)
    whole = ((rows_dev, cols_dev), F32)
    handed = [((row_count, col_count, len(group), piece, band), F32) for group in groups]
    scratch = [vmem((rows_dev, band), F32), pltpu.SemaphoreType.DMA((3,))]
    kernel = functools.partial(first_kernel, groups)
    for_core, for_pair, *here = call(kernel, (smem, vmem, vmem), [block, block, *handed], scratch)(place, recv, eigvecs)

    def operators(number, for_exchange, *known):
        if paired:
            sources = (here[0], there[0]) if number == 0 else (here[0], there[0], here[1], there[1])
            if number == 0:
                odd, even = (((0, 0), (1, 0)), ((1, 0), (0, 0))), ((0, 1), (1, 1))
            else:
                odd, even = (((2, 0), (3, 0)), ((3, 0), (2, 0))), ((1, 1), (0, 1))
        else:
            sources = (recv,)
            odd, even = (((0, 1 + 3 * number),), ((0, 2 + 3 * number),)), ((0, 3 + 3 * number),)
        kernel = functools.partial(operator_kernel, odd, even, for_exchange, len(known))
        weight = ((rows_dev, half * (4 - len(known))), BF16)
        inputs = (place, *sources, *known)
        return call(kernel, (smem,) + (vmem,) * (len(inputs) - 1), [whole, weight, weight])(*inputs)

    def exchange(number, for_core, for_pair):
        from_pair = lax.ppermute(for_pair, "row", pair_route)
        if paired:
            there.append(lax.ppermute(here[number], "col", [(0, 1), (1, 0)]))
            if number == 0:
                for_core, there[number] = lax.optimization_barrier((for_core, there[number]))
        return from_pair, lax.ppermute(for_core, "row", core_route)

    there = []
    from_pair, from_core = exchange(0, for_core, for_pair)
    partial, high, low = operators(0, True, for_core, for_pair)
    for_core, for_pair = call(apply_kernel, (vmem,) * 5, [block] * 2)(high, low, from_pair, from_core, partial)
    from_pair, from_core = exchange(1, for_core, for_pair)
    partial, high, low = operators(1, False, from_core, for_core, for_pair)
    chunks = [vmem(*whole), pltpu.SemaphoreType.DMA((OUT_CHUNKS if cols_dev % (128 * OUT_CHUNKS) == 0 else 1,))]
    return call(last_kernel, (vmem,) * 4, [whole], chunks, pltpu.HBM)(high, low, from_pair, partial)[0]


def solution(mesh):
    in_specs = (P("row", "col"), P(None, "row", "col", None), P(), P())
    return jax.shard_map(on_device, mesh=mesh, in_specs=in_specs, out_specs=P("row", "col"), check_vma=False)
```

```python
import functools

import jax
import jax.numpy as jnp
from jax import lax
from jax.experimental import pallas as pl
from jax.experimental.pallas import tpu as pltpu
from jax.sharding import PartitionSpec as P

F32 = jnp.float32
BF16 = jnp.bfloat16
VMEM_LIMIT = 48 * 1024 * 1024
OUT_CHUNKS = 2


def mxu(a, b):
    return jnp.dot(a, b, preferred_element_type=F32)


def beside(*blocks):
    return jnp.concatenate(blocks, axis=1)


def above(*blocks):
    return jnp.concatenate(blocks, axis=0)


def halves(x):
    high = x.astype(BF16)
    low = (x - high.astype(F32)).astype(BF16)
    return high, low


def thirds(x):
    high = x.astype(BF16)
    rest = x - high.astype(F32)
    middle = rest.astype(BF16)
    return high, middle, (rest - middle.astype(F32)).astype(BF16)


def dot_full(a, b):
    a_high, a_middle, a_low = thirds(a)
    b_high, b_middle, b_low = thirds(b)
    depth, width = b.shape
    small = mxu(beside(a_high, a_low), above(b_low, b_high))
    if depth > 128:
        large = mxu(a_high, beside(b_high, b_middle))
        large += mxu(a_middle, beside(b_high, b_middle))
    elif width > 128:
        left = beside(a_high, a_middle)
        return small + mxu(left, above(b_middle, b_middle)) + mxu(left, above(b_high, b_high))
    else:
        right = beside(b_high, b_middle)
        large = mxu(beside(a_high, a_middle), above(right, right))
    return small + large[:, width:] + large[:, :width]


def dot_split(a, b):
    a_high, a_low = a
    b_high, b_low = b
    if b_high.shape[0] > 128:
        return mxu(a_high, b_low) + mxu(a_low, b_high) + mxu(a_high, b_high)
    return mxu(a_high, b_low) + mxu(beside(a_high, a_low), above(b_high, b_high))


def inverse_factors(grams):
    order = grams[0].shape[0]
    row = lax.broadcasted_iota(jnp.int32, (order, order), 0)
    col = lax.broadcasted_iota(jnp.int32, (order, order), 1)
    diagonal = row == col

    def corner(width):
        same = (row // (2 * width)) == (col // (2 * width))
        return same & ((row // width) % 2 == 0) & ((col // width) % 2 == 1)

    results = []
    for gram in grams:
        kept = jnp.where(diagonal, gram, 0.0)
        inv_col = 2.0 / jnp.sum(kept, axis=1, keepdims=True)
        inv_row = 2.0 / jnp.sum(kept, axis=0, keepdims=True)
        first = jnp.where(corner(1), gram * inv_col * inv_row, 0.0)
        pairs = jnp.where(diagonal, jnp.broadcast_to(inv_row, gram.shape), 0.0) - first
        next_col = jnp.sum(first, axis=1, keepdims=True)
        next_row = jnp.sum(first, axis=0, keepdims=True)
        block = jnp.where(corner(2), gram, 0.0)
        left = inv_col * block - next_col * pltpu.roll(block, order - 1, 0)
        results.append(pairs - (left * inv_row - pltpu.roll(left, 1, 1) * next_row))
    width = 4
    while width < order:
        if 4 * width <= order:
            mask = ((row // (4 * width)) == (col // (4 * width))) & ((row // width) < (col // width))
            inner = [dot_full(x, jnp.where(mask, g, 0.0)) for x, g in zip(results, grams)]
            squares = [dot_full(n, n) for n in inner]
            once = [x - dot_full(n, x) for x, n in zip(results, inner)]
            results = [y + dot_full(n, y) for y, n in zip(once, squares)]
            width *= 4
        else:
            mask = corner(width)
            inner = [dot_full(x, jnp.where(mask, g, 0.0)) for x, g in zip(results, grams)]
            results = [x - dot_full(n, x) for x, n in zip(results, inner)]
            width *= 2
    return results


def wrapped(index, size):
    return jnp.where(index >= size, index - size, index)


def reorder_kernel(layout, shift_ref, group_ref, pieces_ref, out_ref):
    slots = pieces_ref.shape[0]
    for slot in range(slots):
        for sweep, targets in enumerate(layout):
            window = wrapped(group_ref[sweep, slot] + shift_ref[sweep], slots)
            piece = pieces_ref[slot, sweep]
            for block, columns, distance in targets:
                target = wrapped(window + 1, slots) if distance else window
                for c in columns:
                    out_ref[target, c, block] = piece


def fetch_panel(recv_ref, *index):
    rows, cols = recv_ref.shape[:2]
    parts = [recv_ref[(q, c) + index] for c in range(cols) for q in range(rows)]
    return jnp.concatenate(parts, axis=0)


def first_kernel(groups, place_ref, recv_ref, z_ref, core_ref, pair_ref, *refs):
    half = core_ref.shape[0]
    a_ref, sem = refs[-2:]
    copies = []
    for blocks, ref in zip(groups, refs[:-2]):
        for number, block in enumerate(blocks):
            copies.append(pltpu.make_async_copy(recv_ref.at[:, :, block], ref.at[:, :, number], sem.at[len(copies)]))
            copies[-1].start()
    panel = fetch_panel(recv_ref, 0)
    panel_t = panel.T
    gram = dot_full(panel_t, panel)
    projected = halves(dot_split(halves(panel_t), halves(z_ref[...])))
    (inverse,) = inverse_factors([gram])
    a_ref[...] = dot_full(panel, inverse)
    parity = place_ref[0]
    for out_ref, start in ((core_ref, (1 - parity) * half), (pair_ref, parity * half)):
        rows = pl.ds(pl.multiple_of(start, half), half)
        out_ref[...] = z_ref[rows, :] - dot_split(halves(a_ref[rows, :]), projected)
    for copy in copies:
        copy.wait()


def arranged(parity, natural):
    before, top, bottom, after = natural
    even = parity == 0
    return [
        jnp.where(even, before, after),
        jnp.where(even, after, before),
        jnp.where(even, bottom, top),
        jnp.where(even, top, bottom),
    ]


def operator_kernel(odd, even, for_exchange, known, place_ref, *refs):
    partial_ref, high_ref, low_ref = refs[-3:]
    sources, inputs = refs[: -3 - known], refs[-3 - known : -3]
    parity, column = place_ref[0], place_ref[1]

    def panel_of(choices):
        chosen = [fetch_panel(sources[source], block) for source, block in choices]
        return chosen[0] if len(chosen) == 1 else jnp.where(column == 0, chosen[0], chosen[1])

    panels = [panel_of(choices) for choices in (*odd, even)]
    panels_t = [p.T for p in panels]
    size = panels[0].shape[0]
    half = size // 2
    inverses = inverse_factors([dot_full(t, p) for t, p in zip(panels_t, panels)])
    row = lax.broadcasted_iota(jnp.int32, (size, size), 0)
    col = lax.broadcasted_iota(jnp.int32, (size, size), 1)
    identity = jnp.where(row == col, 1.0, 0.0).astype(F32)
    operators = []
    for panel, panel_t, inverse, rows in zip(panels, panels_t, inverses, (slice(0, half), slice(half, size), slice(0, size))):
        scaled = dot_full(panel[rows], inverse)
        operators.append(identity[rows] - dot_full(scaled, panel_t))
    own, other, last = operators
    if for_exchange:
        flipped = parity == 0
        upper, lower = last[:half], last[half:]
        last = jnp.concatenate([jnp.where(flipped, lower, upper), jnp.where(flipped, upper, lower)], axis=0)
    left = dot_split(halves(last[:, :half]), halves(other))
    right = dot_split(halves(last[:, half:]), halves(own))
    natural = (left[:, :half], left[:, half:], right[:, :half], right[:, half:])
    order = arranged(parity, natural)
    high_ref[...], low_ref[...] = halves(beside(*order[: 4 - known]))
    rows = above(*(ref[...] for ref in inputs))
    partial_ref[...] = dot_split(halves(beside(*order[4 - known :])), halves(rows))


def apply_kernel(high_ref, low_ref, pair_in, core_in, partial_ref, core_out, pair_out):
    half = core_out.shape[0]
    total = dot_split((high_ref[...], low_ref[...]), halves(above(pair_in[...], core_in[...]))) + partial_ref[...]
    core_out[...] = total[:half]
    pair_out[...] = total[half:]


def last_kernel(high_ref, low_ref, pair_in, partial_ref, out_ref, result, sems):
    chunk = pair_in.shape[1] // sems.shape[0]
    copies = []
    for number in range(sems.shape[0]):
        at = pl.ds(number * chunk, chunk)
        result[:, at] = dot_split((high_ref[...], low_ref[...]), halves(pair_in[:, at])) + partial_ref[:, at]
        copies.append(pltpu.make_async_copy(result.at[:, at], out_ref.at[:, at], sems.at[number]))
        copies[-1].start()
    for copy in copies:
        copy.wait()


def call(kernel, in_spaces, outs, scratch=(), out_space=pltpu.VMEM):
    return pl.pallas_call(
        kernel,
        in_specs=[pl.BlockSpec(memory_space=space) for space in in_spaces],
        out_specs=[pl.BlockSpec(memory_space=out_space) for _ in outs],
        out_shape=[jax.ShapeDtypeStruct(shape, dtype) for shape, dtype in outs],
        scratch_shapes=list(scratch),
        compiler_params=pltpu.CompilerParams(vmem_limit_bytes=VMEM_LIMIT),
    )


def on_device(eigvecs, panels, sweep_shift, slot_group):
    sweeps, _, panel_rows, band = panels.shape
    rows_dev, cols_dev = eigvecs.shape
    half = rows_dev // 2
    row_count, col_count = lax.axis_size("row"), lax.axis_size("col")
    piece = panel_rows // row_count
    smem, vmem = pltpu.SMEM, pltpu.VMEM
    place = jnp.stack([lax.axis_index("row") % 2, lax.axis_index("col")]).astype(jnp.int32)

    core_route = [(i, i ^ 1) for i in range(row_count)]
    pair_route = [(i, (i + 1 if i % 2 else i - 1) % row_count) for i in range(row_count)]

    panels, place = lax.optimization_barrier((panels, place))
    split = panels.reshape(sweeps, row_count, piece, band).transpose(1, 0, 2, 3)
    pieces = lax.all_to_all(split, "row", 0, 0, tiled=True)
    columns = tuple(range(col_count))
    paired = col_count == 2
    if paired:
        one, two = (0,), (1,)
        layout = (
            ((0, columns, 0),),
            ((1, one, 0), (1, two, 1)),
            ((2, one, 0),),
            ((3, one, 0), (3, two, 1)),
            ((2, two, 0),),
        )
        groups = ((1, 2), (3,))
    else:
        layout = (
            ((0, columns, 0),),
            ((1, columns, 0), (2, columns, 1)),
            ((3, columns, 0),),
            ((4, columns, 0), (5, columns, 1)),
            ((6, columns, 0),),
        )
        groups = ()
    blocks = 1 + max(target[0] for targets in layout for target in targets)
    shape = (row_count, col_count, blocks, piece, band)
    (routed,) = call(
        functools.partial(reorder_kernel, layout),
        (smem, smem, vmem),
        [(shape, F32)],
    )(sweep_shift, slot_group, pieces)
    flat = routed.reshape((row_count * col_count, blocks, piece, band))
    recv = lax.all_to_all(flat, ("row", "col"), 0, 0, tiled=True).reshape(shape)

    block = ((half, cols_dev), F32)
    whole = ((rows_dev, cols_dev), F32)
    handed = [((row_count, col_count, len(group), piece, band), F32) for group in groups]
    scratch = [vmem((rows_dev, band), F32), pltpu.SemaphoreType.DMA((3,))]
    kernel = functools.partial(first_kernel, groups)
    for_core, for_pair, *here = call(kernel, (smem, vmem, vmem), [block, block, *handed], scratch)(place, recv, eigvecs)

    def operators(number, for_exchange, *known):
        if paired:
            sources = (here[0], there[0]) if number == 0 else (here[0], there[0], here[1], there[1])
            if number == 0:
                odd, even = (((0, 0), (1, 0)), ((1, 0), (0, 0))), ((0, 1), (1, 1))
            else:
                odd, even = (((2, 0), (3, 0)), ((3, 0), (2, 0))), ((1, 1), (0, 1))
        else:
            sources = (recv,)
            odd, even = (((0, 1 + 3 * number),), ((0, 2 + 3 * number),)), ((0, 3 + 3 * number),)
        kernel = functools.partial(operator_kernel, odd, even, for_exchange, len(known))
        weight = ((rows_dev, half * (4 - len(known))), BF16)
        inputs = (place, *sources, *known)
        return call(kernel, (smem,) + (vmem,) * (len(inputs) - 1), [whole, weight, weight])(*inputs)

    def exchange(number, for_core, for_pair):
        from_pair = lax.ppermute(for_pair, "row", pair_route)
        if paired:
            there.append(lax.ppermute(here[number], "col", [(0, 1), (1, 0)]))
            if number == 0:
                for_core, there[number] = lax.optimization_barrier((for_core, there[number]))
        return from_pair, lax.ppermute(for_core, "row", core_route)

    there = []
    from_pair, from_core = exchange(0, for_core, for_pair)
    partial, high, low = operators(0, True, for_core, for_pair)
    for_core, for_pair = call(apply_kernel, (vmem,) * 5, [block] * 2)(high, low, from_pair, from_core, partial)
    from_pair, from_core = exchange(1, for_core, for_pair)
    partial, high, low = operators(1, False, from_core, for_core, for_pair)
    chunks = [vmem(*whole), pltpu.SemaphoreType.DMA((OUT_CHUNKS if cols_dev % (128 * OUT_CHUNKS) == 0 else 1,))]
    return call(last_kernel, (vmem,) * 4, [whole], chunks, pltpu.HBM)(high, low, from_pair, partial)[0]


def solution(mesh):
    in_specs = (P("row", "col"), P(None, "row", "col", None), P(), P())
    return jax.shard_map(on_device, mesh=mesh, in_specs=in_specs, out_specs=P("row", "col"), check_vma=False)
```
